32 devices in a mesh: grp: 4 (over z), tp: 8 (over y, x, core).
Axes of the slice: x: 2, y: 2, z: 4, core: 2. Of those that a mesh axis runs over, the one named last changes fastest.
Arguments:
- hidden: bfloat16 [4096, 20480], P('grp', 'tp'), may hold values from -6 to 6
- down_weight: bfloat16 [20480, 8192], P('tp'), may hold values from -0.0625 to 0.0625
- adapter_down_factor: bfloat16 [32, 64, 20480], P('grp', None, 'tp'), may hold values from -0.0390625 to 0.0390625
- adapter_up_factor: bfloat16 [32, 64, 8192], P('grp', None, 'tp'), may hold values from -0.75 to 0.75
- row_tile_adapter: int32 [32], P('grp'), may hold values from 0 to 31, as said below
- adapter_pool_slot: int32 [32], replicated, may hold values from 0 to 31, as said below
Outputs:
- output: bfloat16 [4096, 8192], P('grp', 'tp')
The draws below stay inside these ranges and needn't reach their ends.
Inputs may be any that keep to these rules, and one draw needn't show every extreme that they name: adapter_pool_slot is a permutation; slot s of the pool is held by group s // 8. `row_tile_adapter`: at most 4 tiles of one group have adapters held by one owner group, and in every draw one owner group holds the adapters of exactly 4 tiles of every group.
All inputs are finite; a program needn't handle non-finite values.
Results may differ from the reference program's by a relative error of at most 0.019.
Values may be sent and summed in bfloat16 or wider, within the bound.
No kernel may reach another device: no remote copies, remote signals or barrier semaphores. Data moves between devices by JAX's collectives and lax.ppermute only.
A program may use at most 128 MiB of HBM per device.

```python
import jax
import jax.numpy as jnp
from jax import lax

MODEL_WIDTH = 8192
HIDDEN_SPAN = 20480
ADAPTER_RANK = 64
TILE = 128
TILES_GRP = 8
ADP_GRP = 8
TOKENS = 4096
TILES = 32
ADAPTER_POOL = 32
N_TP = 8


def routing_tables(key):
    group_count = TILES // TILES_GRP
    adapter_slot = jax.random.permutation(jax.random.fold_in(key, 11), ADAPTER_POOL).astype(jnp.int32)
    slot_adapter = jnp.argsort(adapter_slot).astype(jnp.int32)
    hot_owner = jax.random.randint(jax.random.fold_in(key, 12), (), 0, group_count)
    half_count = TILES_GRP // 2
    others = (hot_owner + 1 + jax.random.randint(jax.random.fold_in(key, 13), (group_count, half_count), 0, group_count - 1)) % group_count
    owners = jnp.concatenate([jnp.full((group_count, half_count), hot_owner, jnp.int32), others.astype(jnp.int32)], axis=1)
    scores = jax.random.randint(jax.random.fold_in(key, 14), (group_count, TILES_GRP), 0, 1 << 20) * TILES_GRP + jnp.arange(TILES_GRP, dtype=jnp.int32)[None, :]
    shuffle = jnp.argsort(scores, axis=1)
    owners = jnp.take_along_axis(owners, shuffle, axis=1)
    picked = jax.random.randint(jax.random.fold_in(key, 15), (group_count, TILES_GRP), 0, ADP_GRP)
    tile_table = slot_adapter[owners * ADP_GRP + picked].reshape(group_count * TILES_GRP).astype(jnp.int32)
    return (adapter_slot, tile_table)


def draw_row_tile_adapter(key, part):
    return routing_tables(key)[1]


def draw_adapter_pool_slot(key, part):
    return routing_tables(key)[0]


def spiked(result, own_key, source, target, shards_of, factor):
    def block_of(axis_at):
        return (jnp.arange(result.shape[axis_at]) // (result.shape[axis_at] // shards_of)).reshape((-1,) + (1,) * (result.ndim - 1 - axis_at))

    one_side = jax.random.permutation(own_key, shards_of)[block_of(target)]
    far = (block_of(target) + shards_of // 2) % shards_of
    return jnp.where((block_of(source) == one_side) | (block_of(source) == far), factor * result, result)


def block_levels(own_key, shape, split, low, largest):
    def one(axis_at, blocks):
        heights = jax.random.uniform(jax.random.fold_in(jax.random.fold_in(own_key, 6), axis_at), (blocks,), jnp.float32, low / len(split), largest / len(split))
        return jnp.repeat(jnp.exp(heights), shape[axis_at] // blocks).reshape((-1,) + (1,) * (len(shape) - axis_at - 1))

    factor_of = one(*split[0])
    for cut in split[1:]:
        factor_of = factor_of * one(*cut)
    return factor_of


def bell_draw(rng, dims, deviation, bound, cuts=(), held_as=jnp.bfloat16):
    factor_of = block_levels(rng, dims, cuts, -0.22, 0.18) if cuts else 1.0
    result = jax.random.normal(rng, dims, jnp.float32) * deviation * factor_of
    return jnp.minimum(jnp.maximum(result, -bound), bound).astype(held_as)


def bell_draw_with(own_key, dims, deviation, bound, pieces, heavy, kind=jnp.bfloat16):
    entries = deviation * jax.random.normal(own_key, dims, jnp.float32)
    if pieces:
        entries = entries * block_levels(own_key, dims, pieces, -0.22, 0.18)
    return jnp.clip(spiked(entries, jax.random.fold_in(own_key, 3), *heavy), -bound, bound).astype(kind)


def setup_inputs(seed: int = 0) -> dict:
    key_list = jax.random.split(jax.random.key(seed), 7)
    hidden = bell_draw(key_list[0], (TOKENS, HIDDEN_SPAN), 1.0, 6.0, ((0, 4), (1, 8)))
    down_weight = bell_draw_with(key_list[1], (HIDDEN_SPAN, MODEL_WIDTH), HIDDEN_SPAN ** -0.5, 0.0625, ((0, 8),), (0, 1, 8, 2.0))
    adapter_down_factor = bell_draw(key_list[2], (ADAPTER_POOL, ADAPTER_RANK, HIDDEN_SPAN), HIDDEN_SPAN ** -0.5, 0.0390625, ((0, 4), (2, 8)))
    adapter_up_factor = bell_draw(key_list[3], (ADAPTER_POOL, ADAPTER_RANK, MODEL_WIDTH), ADAPTER_RANK ** -0.5, 0.75, ((0, 4), (2, 8)))
    row_tile_adapter = draw_row_tile_adapter(jax.random.fold_in(key_list[6], 71), 0)
    adapter_pool_slot = draw_adapter_pool_slot(jax.random.fold_in(key_list[6], 71), 0)
    return {"hidden": hidden, "down_weight": down_weight, "adapter_down_factor": adapter_down_factor, "adapter_up_factor": adapter_up_factor, "row_tile_adapter": row_tile_adapter, "adapter_pool_slot": adapter_pool_slot}


adapter_scale = 2.0


def reference(hidden, down_weight, adapter_down_factor, adapter_up_factor, row_tile_adapter, adapter_pool_slot):
    block_width = HIDDEN_SPAN // N_TP

    def accumulate(running, block_index):
        offset_cols = (block_index * block_width).astype(jnp.int32)
        hidden_block = lax.dynamic_slice_in_dim(hidden, offset_cols, block_width, 1)
        weight_rows = lax.dynamic_slice_in_dim(down_weight, offset_cols, block_width, 0)
        partial_value = jnp.dot(hidden_block, weight_rows, preferred_element_type=jnp.float32).astype(jnp.bfloat16)
        return running + partial_value.astype(jnp.float32), None

    base, _ = lax.scan(accumulate, jnp.zeros((TOKENS, MODEL_WIDTH), jnp.float32), jnp.arange(N_TP, dtype=jnp.int32))
    slot_table = adapter_pool_slot[row_tile_adapter].astype(jnp.int32)
    tile_rows = hidden.reshape(TILES, TILE, HIDDEN_SPAN).astype(jnp.float32)
    selected_down = adapter_down_factor[slot_table].astype(jnp.float32)
    rank_projections = jnp.einsum("ktf,krf->ktr", tile_rows, selected_down).astype(jnp.bfloat16)
    selected_up = adapter_up_factor[slot_table].astype(jnp.float32)
    adapted_output = (jnp.einsum("pjf,pfb->pjb", rank_projections.astype(jnp.float32), selected_up) * adapter_scale).astype(jnp.bfloat16)
    return (base + adapted_output.reshape(TOKENS, MODEL_WIDTH).astype(jnp.float32)).astype(jnp.bfloat16)
```

```python
import functools

import jax
import jax.numpy as jnp
from jax import lax
from jax.experimental import pallas as pl
from jax.experimental.pallas import tpu as pltpu
from jax.sharding import PartitionSpec as P

adapter_scale = 2.0
OWNER_CAP = 4
CHUNKS = 2
VMEM_LIMIT = 56 * 1024 * 1024
MiB = 1024 * 1024


def params():
    return pltpu.CompilerParams(vmem_limit_bytes=VMEM_LIMIT)


def gemm_kernel(n_add, n_out, per_out, row_parts, order_ref, hidden_ref, weight_ref, *refs):
    adds, outs, (rows, sems) = refs[:n_add], refs[n_add : n_add + n_out], refs[n_add + n_out :]
    step = pl.program_id(0)
    part = rows.shape[0] // row_parts

    def copy(m):
        span = pl.ds(m * part, part)
        return pltpu.make_async_copy(hidden_ref.at[span], rows.at[span], sems.at[m])

    @pl.when(step == 0)
    def _():
        for m in range(row_parts):
            copy(m).start()

    for m in range(row_parts):
        span = pl.ds(m * part, part)

        @pl.when(step == 0)
        def _():
            copy(m).wait()

        value = jnp.dot(rows[span, :], weight_ref[...], preferred_element_type=jnp.float32)
        for add in adds:
            value = value + add[0, span, :].astype(jnp.float32)
        value = value.astype(jnp.bfloat16)
        for o in range(n_out):
            if n_out == 1:
                outs[o][0, span, :] = value
            else:

                @pl.when(step // per_out == o)
                def _():
                    outs[o][0, span, :] = value


def gemm(hidden, weight, order, width, n_cols, offset, tile, blocks_per_out, adds=()):
    tokens, depth = hidden.shape
    count = order.shape[0]
    tiles = n_cols // tile
    n_out = count // blocks_per_out
    per_out = blocks_per_out * tiles

    def weight_at(i, order_ref):
        return 0, (order_ref[i // tiles] * width + offset) // tile + i % tiles

    def add_at(i, order_ref):
        return i // tiles, 0, i % tiles

    def out_at(o, i, order_ref):
        own = jnp.clip(i - o * per_out, 0, per_out - 1)
        return own // tiles, 0, own % tiles

    row_parts = 4
    total = tokens * depth * n_cols * count
    outs = pl.pallas_call(
        functools.partial(gemm_kernel, len(adds), n_out, per_out, row_parts),
        out_shape=[jax.ShapeDtypeStruct((blocks_per_out, tokens, n_cols), jnp.bfloat16)] * n_out,
        grid_spec=pltpu.PrefetchScalarGridSpec(
            num_scalar_prefetch=1,
            grid=(count * tiles,),
            in_specs=[
                pl.BlockSpec(memory_space=pl.ANY),
                pl.BlockSpec((depth, tile), weight_at),
            ]
            + [pl.BlockSpec((1, tokens, tile), add_at)] * len(adds),
            out_specs=[pl.BlockSpec((1, tokens, tile), functools.partial(out_at, o)) for o in range(n_out)],
            scratch_shapes=[
                pltpu.VMEM((tokens, depth), jnp.bfloat16),
                pltpu.SemaphoreType.DMA((row_parts,)),
            ],
        ),
        compiler_params=params(),
        cost_estimate=pl.CostEstimate(
            flops=2 * total, bytes_accessed=2 * (tokens * depth + count * n_cols * (depth + tokens)), transcendentals=0
        ),
        name="base_products",
    )(order, hidden, weight, *adds)
    return outs


def route_kernel(groups, per_owner, dist, slot_ref, me_ref, down_ref, *refs):
    outs, sems = refs[: len(dist)], refs[len(dist)]
    tiles = slot_ref.shape[1]
    me = me_ref[0]

    def each(act):
        for k, (d, out) in enumerate(zip(dist, outs)):
            other = me + d
            inside = jnp.logical_and(other >= 0, other < groups)
            row = jnp.clip(other, 0, groups - 1)
            seen = jnp.int32(0)
            for i in range(tiles):
                slot = slot_ref[row, i]
                mine = jnp.logical_and(slot // per_owner == me, jnp.logical_and(inside, seen < OWNER_CAP))

                @pl.when(mine)
                def _(slot=slot, seen=seen, out=out, k=k, i=i):
                    act(pltpu.make_async_copy(down_ref.at[slot % per_owner], out.at[seen], sems.at[k, i]))

                seen = seen + mine.astype(jnp.int32)

    each(lambda c: c.start())
    each(lambda c: c.wait())


def route(table, me, factor, dist, groups):
    per_owner, rank, width = factor.shape
    return pl.pallas_call(
        functools.partial(route_kernel, groups, per_owner, dist),
        out_shape=[jax.ShapeDtypeStruct((OWNER_CAP, rank, width), factor.dtype)] * len(dist),
        in_specs=[
            pl.BlockSpec(memory_space=pltpu.SMEM),
            pl.BlockSpec(memory_space=pltpu.SMEM),
            pl.BlockSpec(memory_space=pl.ANY),
        ],
        out_specs=[pl.BlockSpec(memory_space=pl.ANY)] * len(dist),
        scratch_shapes=[pltpu.SemaphoreType.DMA((len(dist), table.shape[1]))],
        compiler_params=params(),
        cost_estimate=pl.CostEstimate(
            flops=0, bytes_accessed=4 * len(dist) * OWNER_CAP * rank * width, transcendentals=0
        ),
        name="adapters_to_send",
    )(table, me, factor)


def fetch(slot_ref, me, per_owner, dist, sources, held, sems, act):
    tiles = slot_ref.shape[1]
    for i in range(tiles):
        slot = slot_ref[me, i]
        owner = slot // per_owner
        place = jnp.int32(0)
        for k in range(i):
            place = place + (slot_ref[me, k] // per_owner == owner).astype(jnp.int32)
        for d, source in zip((0,) + dist, sources):
            @pl.when(me - owner == d)
            def _(d=d, source=source, slot=slot, place=place, i=i):
                at = slot % per_owner if d == 0 else place
                act(i, pltpu.make_async_copy(source.at[at], held.at[i], sems.at[i]))


def rank_kernel(per_owner, dist, slot_ref, me_ref, hidden_ref, *refs):
    sources, (out_ref, held, sems) = refs[: len(dist) + 1], refs[len(dist) + 1 :]
    me = me_ref[0]
    tiles = slot_ref.shape[1]
    rows = hidden_ref.shape[0] // tiles
    fetch(slot_ref, me, per_owner, dist, sources, held, sems, lambda i, c: c.start())
    for i in range(tiles):
        pltpu.make_async_copy(sources[0].at[0], held.at[i], sems.at[i]).wait()
        out_ref[i] = lax.dot_general(
            held[i],
            hidden_ref[pl.ds(i * rows, rows), :],
            (((1,), (1,)), ((), ())),
            preferred_element_type=jnp.float32,
        ).astype(jnp.bfloat16)


def rank_values(table, me, hidden, dist, sources):
    per_owner, rank, width = sources[0].shape
    tiles = table.shape[1]
    rows = hidden.shape[0] // tiles
    return pl.pallas_call(
        functools.partial(rank_kernel, per_owner, dist),
        out_shape=jax.ShapeDtypeStruct((tiles, rank, rows), jnp.bfloat16),
        in_specs=[
            pl.BlockSpec(memory_space=pltpu.SMEM),
            pl.BlockSpec(memory_space=pltpu.SMEM),
            pl.BlockSpec(memory_space=pltpu.VMEM),
        ]
        + [pl.BlockSpec(memory_space=pl.ANY)] * len(sources),
        out_specs=pl.BlockSpec(memory_space=pltpu.VMEM),
        scratch_shapes=[
            pltpu.VMEM((tiles, rank, width), jnp.bfloat16),
            pltpu.SemaphoreType.DMA((tiles,)),
        ],
        compiler_params=params(),
        cost_estimate=pl.CostEstimate(
            flops=8 * hidden.size * rank, bytes_accessed=2 * (hidden.size + tiles * rank * width), transcendentals=0
        ),
        name="rank_values",
    )(table, me, hidden, *sources)


def final_kernel(per_owner, dist, n_add, chunks, slot_ref, me_ref, rank_ref, *refs):
    adds, refs = refs[: n_add * chunks], refs[n_add * chunks :]
    sources, (out_ref, held, sems) = refs[: len(dist) + 1], refs[len(dist) + 1 :]
    step = pl.program_id(0)
    width = out_ref.shape[1] // chunks

    @pl.when(step == 0)
    def _():
        fetch(slot_ref, me_ref[0], per_owner, dist, sources, held, sems, lambda i, c: c.start())

    pltpu.make_async_copy(sources[0].at[0], held.at[step], sems.at[step]).wait()
    adapted = lax.dot_general(
        rank_ref[0], held[step], (((0,), (0,)), ((), ())), preferred_element_type=jnp.float32
    )
    adapted = adapter_scale * adapted
    for c in range(chunks):
        span = pl.ds(c * width, width)
        value = adapted[:, c * width : (c + 1) * width].astype(jnp.bfloat16).astype(jnp.float32)
        for add in adds[c * n_add : (c + 1) * n_add]:
            value = value + add[0].astype(jnp.float32)
        out_ref[:, span] = value.astype(jnp.bfloat16)


def final(table, me, ranks, adds, dist, sources):
    per_owner, rank, width = sources[0].shape
    tiles, _, rows = ranks.shape
    chunks, n_add = len(adds), len(adds[0])
    flat = [a for chunk in adds for a in chunk]
    return pl.pallas_call(
        functools.partial(final_kernel, per_owner, dist, n_add, chunks),
        out_shape=jax.ShapeDtypeStruct((tiles * rows, width), jnp.bfloat16),
        grid=(tiles,),
        in_specs=[
            pl.BlockSpec(memory_space=pltpu.SMEM),
            pl.BlockSpec(memory_space=pltpu.SMEM),
            pl.BlockSpec((1, rank, rows), lambda i: (i, 0, 0)),
        ]
        + [pl.BlockSpec((1, rows, a.shape[2]), lambda i: (0, i, 0)) for a in flat]
        + [pl.BlockSpec(memory_space=pl.ANY)] * len(sources),
        out_specs=pl.BlockSpec((rows, width), lambda i: (i, 0)),
        scratch_shapes=[
            pltpu.VMEM((tiles, rank, width), jnp.bfloat16),
            pltpu.SemaphoreType.DMA((tiles,)),
        ],
        compiler_params=params(),
        cost_estimate=pl.CostEstimate(
            flops=4 * tiles * rows * rank * width,
            bytes_accessed=2 * (len(flat) + 2) * tiles * rows * width // chunks,
            transcendentals=0,
        ),
        name="adapted_and_sum",
    )(table, me, ranks, *flat, *sources)


def local(
    groups,
    n_tp,
    hidden,
    down_weight,
    adapter_down_factor,
    adapter_up_factor,
    row_tile_adapter,
    adapter_pool_slot,
):
    chips = n_tp // 2
    width = down_weight.shape[1] // n_tp
    n_cols = width // CHUNKS
    tile = min(512, n_cols)
    grp, tp = lax.axis_index("grp"), lax.axis_index("tp")
    chip, core = tp // 2, tp % 2
    me = grp.reshape(1).astype(jnp.int32)

    table = adapter_pool_slot[row_tile_adapter].reshape(1, -1).astype(jnp.int32)
    step = 1
    while step < groups:
        other = lax.ppermute(table, "grp", [(g, g ^ step) for g in range(groups)])
        upper = (grp // step) % 2 == 1
        table = jnp.where(
            upper, jnp.concatenate([other, table]), jnp.concatenate([table, other])
        )
        step *= 2

    dist = tuple(d for far in range(groups - 1, 0, -1) for d in (far, -far))

    def send(v, d):
        return lax.ppermute(v, "grp", [(g, g + d) for g in range(groups) if 0 <= g + d < groups])

    down_out = route(table, me, adapter_down_factor, dist, groups)
    down_in = [adapter_down_factor] + [send(v, d) for v, d in zip(down_out, dist)]
    up_out = route(table, me, adapter_up_factor, dist, groups)
    up_in = [adapter_up_factor] + [send(v, d) for v, d in zip(up_out, dist)]

    relative = jnp.array(list(range(1, chips)) + [0], jnp.int32)
    far_chips = (chip ^ relative).astype(jnp.int32)
    theirs, ours = far_chips * 2 + (1 - core), far_chips * 2 + core
    adds = []
    for c in range(CHUNKS):
        (first,) = gemm(hidden, down_weight, theirs, width, n_cols, c * n_cols, tile, chips)
        other = lax.ppermute(first, "tp", [(i, i ^ 1) for i in range(n_tp)])
        sums = gemm(hidden, down_weight, ours, width, n_cols, c * n_cols, tile, 1, (other,))
        got = [
            lax.ppermute(sums[r - 1], "tp", [(i, i ^ (2 * r)) for i in range(n_tp)])
            for r in range(1, chips)
        ]
        adds.append([sums[chips - 1]] + got)

    ranks = rank_values(table, me, hidden, dist, down_in)
    bit = 1
    while bit < n_tp:
        ranks = ranks + lax.ppermute(ranks, "tp", [(i, i ^ bit) for i in range(n_tp)])
        bit *= 2

    return final(table, me, ranks, adds, dist, up_in)


def solution(mesh):
    placed = (
        P("grp", "tp"),
        P("tp", None),
        P("grp", None, "tp"),
        P("grp", None, "tp"),
        P("grp"),
        P(),
    )
    return jax.shard_map(
        functools.partial(local, mesh.shape["grp"], mesh.shape["tp"]),
        mesh=mesh,
        in_specs=placed,
        out_specs=P("grp", "tp"),
        check_vma=False,
    )
```

```python
import functools

import jax
import jax.numpy as jnp
from jax import lax
from jax.experimental import pallas as pl
from jax.experimental.pallas import tpu as pltpu
from jax.sharding import PartitionSpec as P

adapter_scale = 2.0
OWNER_CAP = 4
CHUNKS = 4
UP_GATE = 3
VMEM_LIMIT = 62 * 1024 * 1024


def params():
    return pltpu.CompilerParams(vmem_limit_bytes=VMEM_LIMIT)


def cost(flops, bytes_accessed):
    return pl.CostEstimate(flops=flops, bytes_accessed=bytes_accessed, transcendentals=0)


def after(value, *others):
    return lax.optimization_barrier((value, *others))[0]


def gemm_kernel(n_add, n_out, per_out, row_parts, order_ref, hidden_ref, weight_ref, *refs):
    adds, outs = refs[:n_add], refs[n_add:]
    part = hidden_ref.shape[0] // row_parts

    def products(out):
        for m in range(row_parts):
            span = pl.ds(m * part, part)
            value = jnp.dot(hidden_ref[span, :], weight_ref[...], preferred_element_type=jnp.float32)
            for add in adds:
                value = value + add[0, span, :].astype(jnp.float32)
            out[0, span, :] = value.astype(jnp.bfloat16)

    if n_out == 1:
        products(outs[0])
    else:
        for o in range(n_out):
            pl.when(pl.program_id(0) // per_out == o)(functools.partial(products, outs[o]))


def gemm(hidden, weight, order, width, n_cols, offset, tile, blocks_per_out, adds=()):
    tokens, depth = hidden.shape
    count = order.shape[0]
    tiles = n_cols // tile
    n_out = count // blocks_per_out
    per_out = blocks_per_out * tiles

    def weight_at(i, order_ref):
        return 0, (order_ref[i // tiles] * width + offset) // tile + i % tiles

    def add_at(i, order_ref):
        return i // tiles, 0, i % tiles

    def out_at(o, i, order_ref):
        own = jnp.clip(i - o * per_out, 0, per_out - 1)
        return own // tiles, 0, own % tiles

    row_parts = 4
    total = tokens * depth * n_cols * count
    outs = pl.pallas_call(
        functools.partial(gemm_kernel, len(adds), n_out, per_out, row_parts),
        out_shape=[jax.ShapeDtypeStruct((blocks_per_out, tokens, n_cols), jnp.bfloat16)] * n_out,
        grid_spec=pltpu.PrefetchScalarGridSpec(
            num_scalar_prefetch=1,
            grid=(count * tiles,),
            in_specs=[
                pl.BlockSpec((tokens, depth), lambda i, order_ref: (0, 0)),
                pl.BlockSpec((depth, tile), weight_at),
            ]
            + [pl.BlockSpec((1, tokens, tile), add_at)] * len(adds),
            out_specs=[pl.BlockSpec((1, tokens, tile), functools.partial(out_at, o)) for o in range(n_out)],
        ),
        compiler_params=params(),
        cost_estimate=cost(2 * total, 2 * (tokens * depth + count * n_cols * (depth + tokens))),
        name="base_products",
    )(order, hidden, weight, *adds)
    return outs


def route_kernel(per_owner, slot_ref, me_ref, own_ref, out_ref, sems):
    groups, tiles = slot_ref.shape
    me = me_ref[0]

    def each(act):
        for g in range(groups):
            seen = jnp.int32(0)
            for i in range(tiles):
                slot = slot_ref[g, i]
                mine = jnp.logical_and(slot // per_owner == me, jnp.logical_and(g != me, seen < OWNER_CAP))

                @pl.when(mine)
                def _(slot=slot, seen=seen, g=g, i=i):
                    act(pltpu.make_async_copy(own_ref.at[slot % per_owner], out_ref.at[g, seen], sems.at[g, i]))

                seen = seen + mine.astype(jnp.int32)

    each(lambda c: c.start())
    each(lambda c: c.wait())


def route(table, me, factor):
    per_owner, rank, width = factor.shape
    groups, tiles = table.shape
    return pl.pallas_call(
        functools.partial(route_kernel, per_owner),
        out_shape=jax.ShapeDtypeStruct((groups, OWNER_CAP, rank, width), factor.dtype),
        in_specs=[
            pl.BlockSpec(memory_space=pltpu.SMEM),
            pl.BlockSpec(memory_space=pltpu.SMEM),
            pl.BlockSpec(memory_space=pltpu.VMEM),
        ],
        out_specs=pl.BlockSpec(memory_space=pl.ANY),
        scratch_shapes=[pltpu.SemaphoreType.DMA((groups, tiles))],
        compiler_params=params(),
        cost_estimate=cost(0, 2 * (per_owner + groups * OWNER_CAP) * rank * width),
        name="adapters_to_send",
    )(table, me, factor)


def fetch(slot_ref, me, own_ref, got_ref, held, sems):
    per_owner, tiles = own_ref.shape[0], slot_ref.shape[1]
    for i in range(tiles):
        slot = slot_ref[me, i]
        owner = slot // per_owner
        place = jnp.int32(0)
        for k in range(i):
            place = place + (slot_ref[me, k] // per_owner == owner).astype(jnp.int32)

        @pl.when(owner == me)
        def _(i=i, slot=slot):
            pltpu.make_async_copy(own_ref.at[slot % per_owner], held.at[i], sems.at[i]).start()

        @pl.when(owner != me)
        def _(i=i, owner=owner, place=place):
            pltpu.make_async_copy(got_ref.at[owner, place], held.at[i], sems.at[i]).start()


def rank_kernel(slot_ref, me_ref, hidden_ref, own_ref, got_ref, out_ref, rows_ref, held, row_sems, sems):
    tiles = slot_ref.shape[1]
    rows = rows_ref.shape[1]

    def tile_copy(i):
        return pltpu.make_async_copy(hidden_ref.at[pl.ds(i * rows, rows)], rows_ref.at[i], row_sems.at[i])

    for i in range(tiles):
        tile_copy(i).start()
    fetch(slot_ref, me_ref[0], own_ref, got_ref, held, sems)
    for i in range(tiles):
        tile_copy(i).wait()
        pltpu.make_async_copy(own_ref.at[0], held.at[i], sems.at[i]).wait()
        out_ref[i] = lax.dot_general(
            held[i], rows_ref[i], (((1,), (1,)), ((), ())), preferred_element_type=jnp.float32
        ).astype(jnp.bfloat16)


def rank_values(table, me, hidden, own, got):
    _, rank, width = own.shape
    tiles = table.shape[1]
    rows = hidden.shape[0] // tiles
    return pl.pallas_call(
        rank_kernel,
        out_shape=jax.ShapeDtypeStruct((tiles, rank, rows), jnp.bfloat16),
        in_specs=[pl.BlockSpec(memory_space=pltpu.SMEM)] * 2 + [pl.BlockSpec(memory_space=pl.ANY)] * 3,
        out_specs=pl.BlockSpec(memory_space=pltpu.VMEM),
        scratch_shapes=[
            pltpu.VMEM((tiles, rows, width), jnp.bfloat16),
            pltpu.VMEM((tiles, rank, width), jnp.bfloat16),
            pltpu.SemaphoreType.DMA((tiles,)),
            pltpu.SemaphoreType.DMA((tiles,)),
        ],
        compiler_params=params(),
        cost_estimate=cost(2 * hidden.size * rank, 2 * (hidden.size + tiles * rank * width)),
        name="rank_values",
    )(table, me, hidden, own, got)


def sum_kernel(n_add, *refs):
    out_ref = refs[-1]
    width = out_ref.shape[1] * n_add // (len(refs) - 1)
    for c in range((len(refs) - 1) // n_add):
        adds = refs[c * n_add : (c + 1) * n_add]
        value = adds[0][0].astype(jnp.float32)
        for add in adds[1:]:
            value = value + add[0].astype(jnp.float32)
        out_ref[:, pl.ds(c * width, width)] = value


def sum_base(adds, parts):
    flat = [a for chunk in adds for a in chunk]
    _, tokens, n_cols = flat[0].shape
    rows = tokens // parts
    width = n_cols * len(adds)
    return pl.pallas_call(
        functools.partial(sum_kernel, len(adds[0])),
        out_shape=jax.ShapeDtypeStruct((tokens, width), jnp.float32),
        grid=(parts,),
        in_specs=[pl.BlockSpec((1, rows, n_cols), lambda i: (0, i, 0))] * len(flat),
        out_specs=pl.BlockSpec((rows, width), lambda i: (i, 0)),
        compiler_params=params(),
        cost_estimate=cost(tokens * n_cols * len(flat), tokens * (2 * n_cols * len(flat) + 4 * width)),
        name="base_sum",
    )(*flat)


def final_kernel(per_step, slot_ref, me_ref, base_ref, own_ref, got_ref, *refs):
    ranks, (out_ref, held, sems) = refs[:-3], refs[-3:]
    step = pl.program_id(0)
    rows = ranks[0].shape[2]

    @pl.when(step == 0)
    def _():
        fetch(slot_ref, me_ref[0], own_ref, got_ref, held, sems)

    for t in range(per_step):
        tile = step * per_step + t
        pltpu.make_async_copy(own_ref.at[0], held.at[tile], sems.at[tile]).wait()
        rank = ranks[0][t].astype(jnp.float32)
        for other in ranks[1:]:
            rank = rank + other[t].astype(jnp.float32)
        adapted = lax.dot_general(
            rank.astype(jnp.bfloat16), held[tile], (((0,), (0,)), ((), ())), preferred_element_type=jnp.float32
        )
        adapted = (adapter_scale * adapted).astype(jnp.bfloat16).astype(jnp.float32)
        span = pl.ds(t * rows, rows)
        out_ref[span, :] = (base_ref[span, :] + adapted).astype(jnp.bfloat16)


def final(table, me, ranks, base, own, got):
    _, rank, width = own.shape
    tiles, _, rows = ranks[0].shape
    per_step = 2
    return pl.pallas_call(
        functools.partial(final_kernel, per_step),
        out_shape=jax.ShapeDtypeStruct((tiles * rows, width), jnp.bfloat16),
        grid=(tiles // per_step,),
        in_specs=[
            pl.BlockSpec(memory_space=pltpu.SMEM),
            pl.BlockSpec(memory_space=pltpu.SMEM),
            pl.BlockSpec((per_step * rows, width), lambda i: (i, 0)),
            pl.BlockSpec(memory_space=pl.ANY),
            pl.BlockSpec(memory_space=pl.ANY),
        ]
        + [pl.BlockSpec((per_step, rank, rows), lambda i: (i, 0, 0))] * len(ranks),
        out_specs=pl.BlockSpec((per_step * rows, width), lambda i: (i, 0)),
        scratch_shapes=[
            pltpu.VMEM((tiles, rank, width), jnp.bfloat16),
            pltpu.SemaphoreType.DMA((tiles,)),
        ],
        compiler_params=params(),
        cost_estimate=cost(2 * tiles * rows * rank * width, 6 * tiles * rows * width),
        name="adapted_and_sum",
    )(table, me, base, own, got, *ranks)


def local(
    groups,
    n_tp,
    hidden,
    down_weight,
    adapter_down_factor,
    adapter_up_factor,
    row_tile_adapter,
    adapter_pool_slot,
):
    chips = n_tp // 2
    width = down_weight.shape[1] // n_tp
    chunks = max(1, min(CHUNKS, width // 128))
    n_cols = width // chunks
    tile = min(512, n_cols)
    grp, tp = lax.axis_index("grp"), lax.axis_index("tp")
    chip, core = tp // 2, tp % 2
    me = grp.reshape(1).astype(jnp.int32)

    table = adapter_pool_slot[row_tile_adapter].reshape(1, -1).astype(jnp.int32)
    step = 1
    while step < groups:
        other = lax.ppermute(table, "grp", [(g, g ^ step) for g in range(groups)])
        upper = (grp // step) % 2 == 1
        table = jnp.where(
            upper, jnp.concatenate([other, table]), jnp.concatenate([table, other])
        )
        step *= 2

    def send(v):
        return lax.all_to_all(v, "grp", 0, 0, tiled=True)

    down_out = route(table, me, adapter_down_factor)
    down_in = send(down_out)

    relative = jnp.array(list(range(1, chips)) + [0], jnp.int32)
    far_chips = (chip ^ relative).astype(jnp.int32)
    theirs, ours = far_chips * 2 + (1 - core), far_chips * 2 + core
    done = down_out
    others, adds = {}, []

    def first_core(c, *done):
        (first,) = gemm(hidden, down_weight, after(theirs, *done), width, n_cols, c * n_cols, tile, chips)
        others[c] = lax.ppermute(first, "tp", [(i, i ^ 1) for i in range(n_tp)])
        return first

    done = first_core(0, down_out)
    for c in range(chunks):
        earlier = adds[c - 2] if c >= 2 else []
        if c + 1 < chunks:
            done = first_core(c + 1, done, *earlier)
        sums = gemm(hidden, down_weight, after(ours, done, *earlier), width, n_cols, c * n_cols, tile, 1, (others[c],))
        done = sums[chips - 1]
        got = [
            lax.ppermute(sums[r - 1], "tp", [(i, i ^ (2 * r)) for i in range(n_tp)])
            for r in range(1, chips)
        ]
        adds.append([done] + got)
    up_out = route(after(table, done), me, adapter_up_factor)
    up_in = send(after(up_out, *sum(adds[:-2], []), *adds[-2][:UP_GATE]))

    ranks = rank_values(after(table, up_out), me, hidden, adapter_down_factor, down_in)
    ranks = ranks + lax.ppermute(ranks, "tp", [(i, i ^ 1) for i in range(n_tp)])
    ranks = [ranks] + [lax.ppermute(ranks, "tp", [(i, i ^ (2 * r)) for i in range(n_tp)]) for r in range(1, chips)]

    base = sum_base(adds, table.shape[1])
    return final(table, me, ranks, base, adapter_up_factor, up_in)


def solution(mesh):
    placed = (
        P("grp", "tp"),
        P("tp", None),
        P("grp", None, "tp"),
        P("grp", None, "tp"),
        P("grp"),
        P(),
    )
    return jax.shard_map(
        functools.partial(local, mesh.shape["grp"], mesh.shape["tp"]),
        mesh=mesh,
        in_specs=placed,
        out_specs=P("grp", "tp"),
        check_vma=False,
    )
```

```python
import functools

import jax
import jax.numpy as jnp
from jax import lax
from jax.experimental import pallas as pl
from jax.experimental.pallas import tpu as pltpu
from jax.sharding import PartitionSpec as P

adapter_scale = 2.0
OWNER_CAP = 4
CHUNKS = 4
UP_GATE = 3


def params(mib):
    return pltpu.CompilerParams(vmem_limit_bytes=mib * 1024 * 1024)


def cost(flops, bytes_accessed):
    return pl.CostEstimate(flops=flops, bytes_accessed=bytes_accessed, transcendentals=0)


def after(value, *others):
    return lax.optimization_barrier((value, *others))[0]


def gemm_kernel(n_add, n_out, per_out, row_parts, order_ref, hidden_ref, weight_ref, *refs):
    adds, outs = refs[:n_add], refs[n_add:]
    part = hidden_ref.shape[0] // row_parts

    def products(out):
        for m in range(row_parts):
            span = pl.ds(m * part, part)
            value = jnp.dot(hidden_ref[span, :], weight_ref[...], preferred_element_type=jnp.float32)
            for add in adds:
                value = value + add[0, span, :].astype(jnp.float32)
            out[0, span, :] = value.astype(jnp.bfloat16)

    if n_out == 1:
        products(outs[0])
    else:
        for o in range(n_out):
            pl.when(pl.program_id(0) // per_out == o)(functools.partial(products, outs[o]))


def gemm(hidden, weight, order, width, n_cols, offset, tile, blocks_per_out, adds=()):
    tokens, depth = hidden.shape
    count = order.shape[0]
    tiles = n_cols // tile
    n_out = count // blocks_per_out
    per_out = blocks_per_out * tiles

    def weight_at(i, order_ref):
        return 0, (order_ref[i // tiles] * width + offset) // tile + i % tiles

    def add_at(i, order_ref):
        return i // tiles, 0, i % tiles

    def out_at(o, i, order_ref):
        own = jnp.clip(i - o * per_out, 0, per_out - 1)
        return own // tiles, 0, own % tiles

    row_parts = 4
    total = tokens * depth * n_cols * count
    outs = pl.pallas_call(
        functools.partial(gemm_kernel, len(adds), n_out, per_out, row_parts),
        out_shape=[jax.ShapeDtypeStruct((blocks_per_out, tokens, n_cols), jnp.bfloat16)] * n_out,
        grid_spec=pltpu.PrefetchScalarGridSpec(
            num_scalar_prefetch=1,
            grid=(count * tiles,),
            in_specs=[
                pl.BlockSpec((tokens, depth), lambda i, order_ref: (0, 0), pipeline_mode=pl.Buffered(1)),
                pl.BlockSpec((depth, tile), weight_at),
            ]
            + [pl.BlockSpec((1, tokens, tile), add_at)] * len(adds),
            out_specs=[pl.BlockSpec((1, tokens, tile), functools.partial(out_at, o)) for o in range(n_out)],
        ),
        compiler_params=params(32),
        cost_estimate=cost(2 * total, 2 * (tokens * depth + count * n_cols * (depth + tokens))),
        name="base_products",
    )(order, hidden, weight, *adds)
    return outs


def route_kernel(per_owner, me_ref, pool_ref, *refs):
    tables, (own_ref, out_ref, sems) = refs[:-3], refs[-3:]
    tiles = tables[0].shape[1]
    me = me_ref[0]

    def each(act):
        for r, table in enumerate(tables, 1):
            seen = jnp.int32(0)
            for i in range(tiles):
                slot = pool_ref[table[0, i]]
                mine = jnp.logical_and(slot // per_owner == me, seen < OWNER_CAP)

                @pl.when(mine)
                def _(slot=slot, seen=seen, r=r, i=i):
                    act(pltpu.make_async_copy(own_ref.at[slot % per_owner], out_ref.at[me ^ r, seen], sems.at[r - 1, i]))

                seen = seen + mine.astype(jnp.int32)

    each(lambda c: c.start())
    each(lambda c: c.wait())


def route(me, pool, tables, factor):
    per_owner, rank, width = factor.shape
    groups = len(tables) + 1
    return pl.pallas_call(
        functools.partial(route_kernel, per_owner),
        out_shape=jax.ShapeDtypeStruct((groups, OWNER_CAP, rank, width), factor.dtype),
        in_specs=[pl.BlockSpec(memory_space=pltpu.SMEM)] * (groups + 1) + [pl.BlockSpec(memory_space=pltpu.VMEM)],
        out_specs=pl.BlockSpec(memory_space=pl.ANY),
        scratch_shapes=[pltpu.SemaphoreType.DMA((groups - 1, tables[0].shape[1]))],
        compiler_params=params(62),
        cost_estimate=cost(0, 2 * (per_owner + groups * OWNER_CAP) * rank * width),
        name="adapters_to_send",
    )(me, pool, *tables, factor)


def fetch(me_ref, pool_ref, own_table, own_ref, got_ref, held, sems):
    per_owner, tiles = own_ref.shape[0], own_table.shape[1]
    slots = [pool_ref[own_table[0, i]] for i in range(tiles)]
    me = me_ref[0]
    for i in range(tiles):
        owner = slots[i] // per_owner
        place = jnp.int32(0)
        for k in range(i):
            place = place + (slots[k] // per_owner == owner).astype(jnp.int32)

        @pl.when(owner == me)
        def _(i=i):
            pltpu.make_async_copy(own_ref.at[slots[i] % per_owner], held.at[i], sems.at[i]).start()

        @pl.when(owner != me)
        def _(i=i, owner=owner, place=place):
            pltpu.make_async_copy(got_ref.at[owner, place], held.at[i], sems.at[i]).start()


def rank_kernel(me_ref, pool_ref, own_table, hidden_ref, own_ref, got_ref, out_ref, rows_ref, held, row_sems, sems):
    tiles = own_table.shape[1]
    rows = rows_ref.shape[1]

    def tile_copy(i):
        return pltpu.make_async_copy(hidden_ref.at[pl.ds(i * rows, rows)], rows_ref.at[i], row_sems.at[i])

    for i in range(tiles):
        tile_copy(i).start()
    fetch(me_ref, pool_ref, own_table, own_ref, got_ref, held, sems)
    for i in range(tiles):
        tile_copy(i).wait()
        pltpu.make_async_copy(own_ref.at[0], held.at[i], sems.at[i]).wait()
        out_ref[i] = lax.dot_general(
            held[i], rows_ref[i], (((1,), (1,)), ((), ())), preferred_element_type=jnp.float32
        ).astype(jnp.bfloat16)


def rank_values(me, pool, table, hidden, own, got):
    _, rank, width = own.shape
    tiles = table.shape[1]
    rows = hidden.shape[0] // tiles
    return pl.pallas_call(
        rank_kernel,
        out_shape=jax.ShapeDtypeStruct((tiles, rank, rows), jnp.bfloat16),
        in_specs=[pl.BlockSpec(memory_space=pltpu.SMEM)] * 3 + [pl.BlockSpec(memory_space=pl.ANY)] * 3,
        out_specs=pl.BlockSpec(memory_space=pltpu.VMEM),
        scratch_shapes=[
            pltpu.VMEM((tiles, rows, width), jnp.bfloat16),
            pltpu.VMEM((tiles, rank, width), jnp.bfloat16),
            pltpu.SemaphoreType.DMA((tiles,)),
            pltpu.SemaphoreType.DMA((tiles,)),
        ],
        compiler_params=params(62),
        cost_estimate=cost(2 * hidden.size * rank, 2 * (hidden.size + tiles * rank * width)),
        name="rank_values",
    )(me, pool, table, hidden, own, got)


def sum_kernel(n_add, *refs):
    out_ref = refs[-1]
    width = out_ref.shape[1] * n_add // (len(refs) - 1)
    for c in range((len(refs) - 1) // n_add):
        adds = refs[c * n_add : (c + 1) * n_add]
        value = adds[0][0].astype(jnp.float32)
        for add in adds[1:]:
            value = value + add[0].astype(jnp.float32)
        out_ref[:, pl.ds(c * width, width)] = value


def sum_base(adds, parts):
    flat = [a for chunk in adds for a in chunk]
    _, tokens, n_cols = flat[0].shape
    rows = tokens // parts
    width = n_cols * len(adds)
    return pl.pallas_call(
        functools.partial(sum_kernel, len(adds[0])),
        out_shape=jax.ShapeDtypeStruct((tokens, width), jnp.float32),
        grid=(parts,),
        in_specs=[pl.BlockSpec((1, rows, n_cols), lambda i: (0, i, 0))] * len(flat),
        out_specs=pl.BlockSpec((rows, width), lambda i: (i, 0)),
        compiler_params=params(62),
        cost_estimate=cost(tokens * n_cols * len(flat), tokens * (2 * n_cols * len(flat) + 4 * width)),
        name="base_sum",
    )(*flat)


def final_kernel(per_step, n_add, me_ref, pool_ref, own_table, *refs):
    base_ref, own_ref, got_ref = refs[:3]
    adds, ranks, (out_ref, held, sems) = refs[3 : 3 + n_add], refs[3 + n_add : -3], refs[-3:]
    step = pl.program_id(0)
    rows = ranks[0].shape[2]
    summed = base_ref.shape[1]

    @pl.when(step == 0)
    def _():
        fetch(me_ref, pool_ref, own_table, own_ref, got_ref, held, sems)

    for t in range(per_step):
        tile = step * per_step + t
        span = pl.ds(t * rows, rows)
        rank = ranks[0][t].astype(jnp.float32)
        for other in ranks[1:]:
            rank = rank + other[t].astype(jnp.float32)
        rank = rank.astype(jnp.bfloat16)
        last = adds[0][0, span, :].astype(jnp.float32)
        for add in adds[1:]:
            last = last + add[0, span, :].astype(jnp.float32)
        pltpu.make_async_copy(own_ref.at[0], held.at[tile], sems.at[tile]).wait()
        adapted = lax.dot_general(rank, held[tile], (((0,), (0,)), ((), ())), preferred_element_type=jnp.float32)
        adapted = (adapter_scale * adapted).astype(jnp.bfloat16).astype(jnp.float32)
        out_ref[span, pl.ds(0, summed)] = (base_ref[span, :] + adapted[:, :summed]).astype(jnp.bfloat16)
        out_ref[span, pl.ds(summed, last.shape[1])] = (last + adapted[:, summed:]).astype(jnp.bfloat16)


def final(me, pool, table, ranks, base, adds, own, got):
    _, rank, width = own.shape
    tiles, _, rows = ranks[0].shape
    per_step = 4
    step_rows = per_step * rows
    return pl.pallas_call(
        functools.partial(final_kernel, per_step, len(adds)),
        out_shape=jax.ShapeDtypeStruct((tiles * rows, width), jnp.bfloat16),
        grid=(tiles // per_step,),
        in_specs=[pl.BlockSpec(memory_space=pltpu.SMEM)] * 3
        + [pl.BlockSpec((step_rows, base.shape[1]), lambda i: (i, 0))]
        + [pl.BlockSpec(memory_space=pl.ANY)] * 2
        + [pl.BlockSpec((1, step_rows, a.shape[2]), lambda i: (0, i, 0)) for a in adds]
        + [pl.BlockSpec((per_step, rank, rows), lambda i: (i, 0, 0))] * len(ranks),
        out_specs=pl.BlockSpec((step_rows, width), lambda i: (i, 0)),
        scratch_shapes=[
            pltpu.VMEM((tiles, rank, width), jnp.bfloat16),
            pltpu.SemaphoreType.DMA((tiles,)),
        ],
        compiler_params=params(62),
        cost_estimate=cost(2 * tiles * rows * rank * width, 6 * tiles * rows * width),
        name="adapted_and_sum",
    )(me, pool, table, base, own, got, *adds, *ranks)


def local(
    groups,
    n_tp,
    hidden,
    down_weight,
    adapter_down_factor,
    adapter_up_factor,
    row_tile_adapter,
    adapter_pool_slot,
):
    chips = n_tp // 2
    width = down_weight.shape[1] // n_tp
    chunks = max(1, min(CHUNKS, width // 128))
    n_cols = width // chunks
    tile = min(512, n_cols)
    grp, tp = lax.axis_index("grp"), lax.axis_index("tp")
    chip, core = tp // 2, tp % 2
    me = grp.reshape(1).astype(jnp.int32)

    pool = adapter_pool_slot.astype(jnp.int32)
    own_table = row_tile_adapter.reshape(1, -1).astype(jnp.int32)
    tables = [lax.ppermute(own_table, "grp", [(g, g ^ r) for g in range(groups)]) for r in range(1, groups)]

    def send(v):
        return lax.all_to_all(v, "grp", 0, 0, tiled=True)

    down_out = route(me, pool, tables, adapter_down_factor)
    down_in = send(down_out)

    relative = jnp.array(list(range(1, chips)) + [0], jnp.int32)
    far_chips = (chip ^ relative).astype(jnp.int32)
    theirs, ours = far_chips * 2 + (1 - core), far_chips * 2 + core
    done = down_out
    others, adds = {}, []

    def first_core(c, *done):
        (first,) = gemm(hidden, down_weight, after(theirs, *done), width, n_cols, c * n_cols, tile, chips)
        others[c] = lax.ppermute(first, "tp", [(i, i ^ 1) for i in range(n_tp)])
        return first

    done = first_core(0, down_out)
    for c in range(chunks):
        earlier = adds[c - 2] if c >= 2 else []
        if c + 1 < chunks:
            done = first_core(c + 1, done, *earlier)
        if c == chunks - 1:
            up_out = route(after(me, done), pool, tables, adapter_up_factor)
            done = up_out
        sums = gemm(hidden, down_weight, after(ours, done, *earlier), width, n_cols, c * n_cols, tile, 1, (others[c],))
        done = sums[chips - 1]
        got = [
            lax.ppermute(sums[r - 1], "tp", [(i, i ^ (2 * r)) for i in range(n_tp)])
            for r in range(1, chips)
        ]
        adds.append([done] + got)
    up_in = send(after(up_out, done, *sum(adds[:-2], []), *adds[-2][:UP_GATE]))

    ranks = rank_values(after(me, done), pool, own_table, hidden, adapter_down_factor, down_in)
    ranks = ranks + lax.ppermute(ranks, "tp", [(i, i ^ 1) for i in range(n_tp)])
    ranks = [ranks] + [lax.ppermute(ranks, "tp", [(i, i ^ (2 * r)) for i in range(n_tp)]) for r in range(1, chips)]

    base = sum_base(adds[:-1], own_table.shape[1])
    return final(me, pool, own_table, ranks, base, adds[-1], adapter_up_factor, up_in)


def solution(mesh):
    placed = (
        P("grp", "tp"),
        P("tp", None),
        P("grp", None, "tp"),
        P("grp", None, "tp"),
        P("grp"),
        P(),
    )
    return jax.shard_map(
        functools.partial(local, mesh.shape["grp"], mesh.shape["tp"]),
        mesh=mesh,
        in_specs=placed,
        out_specs=P("grp", "tp"),
        check_vma=False,
    )
```

```python
import functools

import jax
import jax.numpy as jnp
from jax import lax
from jax.experimental import pallas as pl
from jax.experimental.pallas import tpu as pltpu
from jax.sharding import PartitionSpec as P

adapter_scale = 2.0
OWNER_CAP = 4
CHUNKS = 4
UP_GATE = 3


def params(mib):
    return pltpu.CompilerParams(vmem_limit_bytes=mib * 1024 * 1024)


def cost(flops, bytes_accessed):
    return pl.CostEstimate(flops=flops, bytes_accessed=bytes_accessed, transcendentals=0)


def after(value, *others):
    return lax.optimization_barrier((value, *others))[0]


def gemm_kernel(n_add, n_out, per_out, row_parts, order_ref, hidden_ref, weight_ref, *refs):
    adds, outs = refs[:n_add], refs[n_add:]
    part = hidden_ref.shape[0] // row_parts

    def products(out):
        for m in range(row_parts):
            span = pl.ds(m * part, part)
            value = jnp.dot(hidden_ref[span, :], weight_ref[...], preferred_element_type=jnp.float32)
            for add in adds:
                value = value + add[0, span, :].astype(jnp.float32)
            out[0, span, :] = value.astype(jnp.bfloat16)

    if n_out == 1:
        products(outs[0])
    else:
        for o in range(n_out):
            pl.when(pl.program_id(0) // per_out == o)(functools.partial(products, outs[o]))


def gemm(hidden, weight, order, width, n_cols, offset, tile, blocks_per_out, adds=()):
    tokens, depth = hidden.shape
    count = order.shape[0]
    tiles = n_cols // tile
    n_out = count // blocks_per_out
    per_out = blocks_per_out * tiles

    def weight_at(i, order_ref):
        return 0, (order_ref[i // tiles] * width + offset) // tile + i % tiles

    def add_at(i, order_ref):
        return i // tiles, 0, i % tiles

    def out_at(o, i, order_ref):
        own = jnp.clip(i - o * per_out, 0, per_out - 1)
        return own // tiles, 0, own % tiles

    row_parts = 4
    total = tokens * depth * n_cols * count
    outs = pl.pallas_call(
        functools.partial(gemm_kernel, len(adds), n_out, per_out, row_parts),
        out_shape=[jax.ShapeDtypeStruct((blocks_per_out, tokens, n_cols), jnp.bfloat16)] * n_out,
        grid_spec=pltpu.PrefetchScalarGridSpec(
            num_scalar_prefetch=1,
            grid=(count * tiles,),
            in_specs=[
                pl.BlockSpec((tokens, depth), lambda i, order_ref: (0, 0), pipeline_mode=pl.Buffered(1)),
                pl.BlockSpec((depth, tile), weight_at),
            ]
            + [pl.BlockSpec((1, tokens, tile), add_at)] * len(adds),
            out_specs=[pl.BlockSpec((1, tokens, tile), functools.partial(out_at, o)) for o in range(n_out)],
        ),
        compiler_params=params(32),
        cost_estimate=cost(2 * total, 2 * (tokens * depth + count * n_cols * (depth + tokens))),
        name="base_products",
    )(order, hidden, weight, *adds)
    return outs


def route_kernel(per_owner, me_ref, pool_ref, *refs):
    tables, (own_ref, out_ref, sems) = refs[:-3], refs[-3:]
    tiles = tables[0].shape[1]
    me = me_ref[0]

    def each(act):
        for r, table in enumerate(tables, 1):
            seen = jnp.int32(0)
            for i in range(tiles):
                slot = pool_ref[table[0, i]]
                mine = jnp.logical_and(slot // per_owner == me, seen < OWNER_CAP)

                @pl.when(mine)
                def _(slot=slot, seen=seen, r=r, i=i):
                    act(pltpu.make_async_copy(own_ref.at[slot % per_owner], out_ref.at[me ^ r, seen], sems.at[r - 1, i]))

                seen = seen + mine.astype(jnp.int32)

    each(lambda c: c.start())
    each(lambda c: c.wait())


def route(me, pool, tables, factor):
    per_owner, rank, width = factor.shape
    groups = len(tables) + 1
    return pl.pallas_call(
        functools.partial(route_kernel, per_owner),
        out_shape=jax.ShapeDtypeStruct((groups, OWNER_CAP, rank, width), factor.dtype),
        in_specs=[pl.BlockSpec(memory_space=pltpu.SMEM)] * (groups + 1) + [pl.BlockSpec(memory_space=pltpu.VMEM)],
        out_specs=pl.BlockSpec(memory_space=pl.ANY),
        scratch_shapes=[pltpu.SemaphoreType.DMA((groups - 1, tables[0].shape[1]))],
        compiler_params=params(62),
        cost_estimate=cost(0, 2 * (per_owner + groups * OWNER_CAP) * rank * width),
        name="adapters_to_send",
    )(me, pool, *tables, factor)


def fetch(me_ref, pool_ref, own_table, own_ref, got_ref, held, sems):
    per_owner, tiles = own_ref.shape[0], own_table.shape[1]
    slots = [pool_ref[own_table[0, i]] for i in range(tiles)]
    me = me_ref[0]
    for i in range(tiles):
        owner = slots[i] // per_owner
        place = jnp.int32(0)
        for k in range(i):
            place = place + (slots[k] // per_owner == owner).astype(jnp.int32)

        @pl.when(owner == me)
        def _(i=i):
            pltpu.make_async_copy(own_ref.at[slots[i] % per_owner], held.at[i], sems.at[i]).start()

        @pl.when(owner != me)
        def _(i=i, owner=owner, place=place):
            pltpu.make_async_copy(got_ref.at[owner, place], held.at[i], sems.at[i]).start()


def rank_kernel(me_ref, pool_ref, own_table, hidden_ref, own_ref, got_ref, out_ref, rows_ref, held, row_sems, sems):
    tiles = own_table.shape[1]
    rows = rows_ref.shape[1]

    def tile_copy(i):
        return pltpu.make_async_copy(hidden_ref.at[pl.ds(i * rows, rows)], rows_ref.at[i], row_sems.at[i])

    for i in range(tiles):
        tile_copy(i).start()
    fetch(me_ref, pool_ref, own_table, own_ref, got_ref, held, sems)
    for i in range(tiles):
        tile_copy(i).wait()
        pltpu.make_async_copy(own_ref.at[0], held.at[i], sems.at[i]).wait()
        out_ref[i] = lax.dot_general(
            held[i], rows_ref[i], (((1,), (1,)), ((), ())), preferred_element_type=jnp.float32
        ).astype(jnp.bfloat16)


def rank_values(me, pool, table, hidden, own, got):
    _, rank, width = own.shape
    tiles = table.shape[1]
    rows = hidden.shape[0] // tiles
    return pl.pallas_call(
        rank_kernel,
        out_shape=jax.ShapeDtypeStruct((tiles, rank, rows), jnp.bfloat16),
        in_specs=[pl.BlockSpec(memory_space=pltpu.SMEM)] * 3 + [pl.BlockSpec(memory_space=pl.ANY)] * 3,
        out_specs=pl.BlockSpec(memory_space=pltpu.VMEM),
        scratch_shapes=[
            pltpu.VMEM((tiles, rows, width), jnp.bfloat16),
            pltpu.VMEM((tiles, rank, width), jnp.bfloat16),
            pltpu.SemaphoreType.DMA((tiles,)),
            pltpu.SemaphoreType.DMA((tiles,)),
        ],
        compiler_params=params(62),
        cost_estimate=cost(2 * hidden.size * rank, 2 * (hidden.size + tiles * rank * width)),
        name="rank_values",
    )(me, pool, table, hidden, own, got)


def sum_kernel(n_add, chunks, *refs):
    adds, out_ref = refs[: n_add * chunks], refs[-1] if len(refs) == n_add * chunks + 1 else refs[-2]
    width = adds[0].shape[2]
    for c in range(chunks):
        value = adds[c * n_add][0].astype(jnp.float32)
        for add in adds[c * n_add + 1 : (c + 1) * n_add]:
            value = value + add[0].astype(jnp.float32)
        out_ref[:, pl.ds(c * width, width)] = value
    if len(refs) > n_add * chunks + 1:
        ranks, rank_ref = refs[n_add * chunks : -2], refs[-1]
        for t in range(rank_ref.shape[0]):
            rank = ranks[0][t].astype(jnp.float32)
            for other in ranks[1:]:
                rank = rank + other[t].astype(jnp.float32)
            rank_ref[t] = rank.astype(jnp.bfloat16).T


def sum_base(adds, tiles, per_step, ranks=()):
    flat = [a for chunk in adds for a in chunk]
    _, tokens, n_cols = flat[0].shape
    steps = tiles // per_step
    rows = tokens // steps
    width = n_cols * len(adds)
    out_shape = [jax.ShapeDtypeStruct((tokens, width), jnp.float32)]
    out_specs = [pl.BlockSpec((rows, width), lambda i: (i, 0))]
    rank_specs = []
    for part in ranks:
        rank_specs.append(pl.BlockSpec((per_step, *part.shape[1:]), lambda i: (i, 0, 0)))
    if ranks:
        _, rank, tile = ranks[0].shape
        out_shape.append(jax.ShapeDtypeStruct((tiles, tile, rank), jnp.bfloat16))
        out_specs.append(pl.BlockSpec((per_step, tile, rank), lambda i: (i, 0, 0)))
    return pl.pallas_call(
        functools.partial(sum_kernel, len(adds[0]), len(adds)),
        out_shape=out_shape,
        grid=(steps,),
        in_specs=[pl.BlockSpec((1, rows, n_cols), lambda i: (0, i, 0))] * len(flat) + rank_specs,
        out_specs=out_specs,
        compiler_params=params(62),
        cost_estimate=cost(tokens * n_cols * len(flat), tokens * (2 * n_cols * len(flat) + 4 * width)),
        name="base_sum",
    )(*flat, *ranks)


def final_kernel(per_step, me_ref, pool_ref, own_table, base_ref, last_ref, rank_ref, own_ref, got_ref, out_ref, held, sems):
    step = pl.program_id(0)
    rows = rank_ref.shape[1]
    summed = base_ref.shape[1]

    @pl.when(step == 0)
    def _():
        fetch(me_ref, pool_ref, own_table, own_ref, got_ref, held, sems)

    for t in range(per_step):
        tile = step * per_step + t
        span = pl.ds(t * rows, rows)
        pltpu.make_async_copy(own_ref.at[0], held.at[tile], sems.at[tile]).wait()
        adapted = jnp.dot(rank_ref[t], held[tile], preferred_element_type=jnp.float32)
        adapted = (adapter_scale * adapted).astype(jnp.bfloat16).astype(jnp.float32)
        out_ref[span, pl.ds(0, summed)] = (base_ref[span, :] + adapted[:, :summed]).astype(jnp.bfloat16)
        rest = last_ref[span, :] + adapted[:, summed:]
        out_ref[span, pl.ds(summed, rest.shape[1])] = rest.astype(jnp.bfloat16)


def final(me, pool, table, ranks, base, last, own, got):
    _, rank, width = own.shape
    tiles, rows, _ = ranks.shape
    per_step = 4
    step_rows = per_step * rows
    return pl.pallas_call(
        functools.partial(final_kernel, per_step),
        out_shape=jax.ShapeDtypeStruct((tiles * rows, width), jnp.bfloat16),
        grid=(tiles // per_step,),
        in_specs=[pl.BlockSpec(memory_space=pltpu.SMEM)] * 3
        + [pl.BlockSpec((step_rows, a.shape[1]), lambda i: (i, 0)) for a in (base, last)]
        + [pl.BlockSpec((per_step, rows, rank), lambda i: (i, 0, 0))]
        + [pl.BlockSpec(memory_space=pl.ANY)] * 2,
        out_specs=pl.BlockSpec((step_rows, width), lambda i: (i, 0)),
        scratch_shapes=[
            pltpu.VMEM((tiles, rank, width), jnp.bfloat16),
            pltpu.SemaphoreType.DMA((tiles,)),
        ],
        compiler_params=params(62),
        cost_estimate=cost(2 * tiles * rows * rank * width, 6 * tiles * rows * width),
        name="adapted_and_sum",
    )(me, pool, table, base, last, ranks, own, got)


def local(
    groups,
    n_tp,
    hidden,
    down_weight,
    adapter_down_factor,
    adapter_up_factor,
    row_tile_adapter,
    adapter_pool_slot,
):
    chips = n_tp // 2
    width = down_weight.shape[1] // n_tp
    chunks = max(1, min(CHUNKS, width // 128))
    n_cols = width // chunks
    tile = min(512, n_cols)
    grp, tp = lax.axis_index("grp"), lax.axis_index("tp")
    chip, core = tp // 2, tp % 2
    me = grp.reshape(1).astype(jnp.int32)

    pool = adapter_pool_slot.astype(jnp.int32)
    own_table = row_tile_adapter.reshape(1, -1).astype(jnp.int32)
    tables = [lax.ppermute(own_table, "grp", [(g, g ^ r) for g in range(groups)]) for r in range(1, groups)]

    def send(v):
        return lax.all_to_all(v, "grp", 0, 0, tiled=True)

    down_out = route(me, pool, tables, adapter_down_factor)
    down_in = send(down_out)

    relative = jnp.array(list(range(1, chips)) + [0], jnp.int32)
    far_chips = (chip ^ relative).astype(jnp.int32)
    theirs, ours = far_chips * 2 + (1 - core), far_chips * 2 + core
    done = down_out
    others, adds = {}, []

    def first_core(c, *done):
        (first,) = gemm(hidden, down_weight, after(theirs, *done), width, n_cols, c * n_cols, tile, chips)
        others[c] = lax.ppermute(first, "tp", [(i, i ^ 1) for i in range(n_tp)])
        return first

    done = first_core(0, down_out)
    for c in range(chunks):
        earlier = adds[c - 2] if c >= 2 else []
        if c + 1 < chunks:
            done = first_core(c + 1, done, *earlier)
        if c == chunks - 1:
            up_out = route(after(me, done), pool, tables, adapter_up_factor)
            done = up_out
        sums = gemm(hidden, down_weight, after(ours, done, *earlier), width, n_cols, c * n_cols, tile, 1, (others[c],))
        done = sums[chips - 1]
        got = [
            lax.ppermute(sums[r - 1], "tp", [(i, i ^ (2 * r)) for i in range(n_tp)])
            for r in range(1, chips)
        ]
        adds.append([done] + got)
    up_in = send(after(up_out, done, *sum(adds[:-2], []), *adds[-2][:UP_GATE]))

    ranks = rank_values(after(me, done), pool, own_table, hidden, adapter_down_factor, down_in)
    ranks = ranks + lax.ppermute(ranks, "tp", [(i, i ^ 1) for i in range(n_tp)])
    ranks = [ranks] + [lax.ppermute(ranks, "tp", [(i, i ^ (2 * r)) for i in range(n_tp)]) for r in range(1, chips)]

    tiles = own_table.shape[1]
    (base,) = sum_base(adds[:-1], tiles, 2)
    last, ranks = sum_base(adds[-1:], tiles, 4, ranks)
    return final(me, pool, own_table, ranks, base, last, adapter_up_factor, up_in)


def solution(mesh):
    placed = (
        P("grp", "tp"),
        P("tp", None),
        P("grp", None, "tp"),
        P("grp", None, "tp"),
        P("grp"),
        P(),
    )
    return jax.shard_map(
        functools.partial(local, mesh.shape["grp"], mesh.shape["tp"]),
        mesh=mesh,
        in_specs=placed,
        out_specs=P("grp", "tp"),
        check_vma=False,
    )
```

```python
import functools

import jax
import jax.numpy as jnp
from jax import lax
from jax.experimental import pallas as pl
from jax.experimental.pallas import tpu as pltpu
from jax.sharding import PartitionSpec as P

adapter_scale = 2.0
OWNER_CAP = 4
CHUNKS = 4
UP_GATE = 3


def params(mib):
    return pltpu.CompilerParams(vmem_limit_bytes=mib * 1024 * 1024)


def cost(flops, bytes_accessed):
    return pl.CostEstimate(flops=flops, bytes_accessed=bytes_accessed, transcendentals=0)


def after(value, *others):
    return lax.optimization_barrier((value, *others))[0]


def gemm_kernel(n_add, n_out, per_out, row_parts, order_ref, hidden_ref, weight_ref, *refs):
    adds, outs = refs[:n_add], refs[n_add:]
    part = hidden_ref.shape[0] // row_parts

    def products(out):
        for m in range(row_parts):
            span = pl.ds(m * part, part)
            value = jnp.dot(hidden_ref[span, :], weight_ref[...], preferred_element_type=jnp.float32)
            for add in adds:
                value = value + add[0, span, :].astype(jnp.float32)
            out[0, span, :] = value.astype(jnp.bfloat16)

    if n_out == 1:
        products(outs[0])
    else:
        for o in range(n_out):
            pl.when(pl.program_id(0) // per_out == o)(functools.partial(products, outs[o]))


def gemm(hidden, weight, order, width, n_cols, offset, tile, blocks_per_out, adds=()):
    tokens, depth = hidden.shape
    count = order.shape[0]
    tiles = n_cols // tile
    n_out = count // blocks_per_out
    per_out = blocks_per_out * tiles

    def weight_at(i, order_ref):
        return 0, (order_ref[i // tiles] * width + offset) // tile + i % tiles

    def add_at(i, order_ref):
        return i // tiles, 0, i % tiles

    def out_at(o, i, order_ref):
        own = jnp.clip(i - o * per_out, 0, per_out - 1)
        return own // tiles, 0, own % tiles

    row_parts = 4
    total = tokens * depth * n_cols * count
    outs = pl.pallas_call(
        functools.partial(gemm_kernel, len(adds), n_out, per_out, row_parts),
        out_shape=[jax.ShapeDtypeStruct((blocks_per_out, tokens, n_cols), jnp.bfloat16)] * n_out,
        grid_spec=pltpu.PrefetchScalarGridSpec(
            num_scalar_prefetch=1,
            grid=(count * tiles,),
            in_specs=[
                pl.BlockSpec((tokens, depth), lambda i, order_ref: (0, 0), pipeline_mode=pl.Buffered(1)),
                pl.BlockSpec((depth, tile), weight_at),
            ]
            + [pl.BlockSpec((1, tokens, tile), add_at)] * len(adds),
            out_specs=[pl.BlockSpec((1, tokens, tile), functools.partial(out_at, o)) for o in range(n_out)],
        ),
        compiler_params=params(32),
        cost_estimate=cost(2 * total, 2 * (tokens * depth + count * n_cols * (depth + tokens))),
        name="base_products",
    )(order, hidden, weight, *adds)
    return outs


def route_kernel(per_owner, me_ref, pool_ref, *refs):
    tables, (own_ref, out_ref, sems) = refs[:-3], refs[-3:]
    tiles = tables[0].shape[1]
    me = me_ref[0]

    def each(act):
        for r, table in enumerate(tables, 1):
            seen = jnp.int32(0)
            for i in range(tiles):
                slot = pool_ref[table[0, i]]
                mine = jnp.logical_and(slot // per_owner == me, seen < OWNER_CAP)

                @pl.when(mine)
                def _(slot=slot, seen=seen, r=r, i=i):
                    act(pltpu.make_async_copy(own_ref.at[slot % per_owner], out_ref.at[me ^ r, seen], sems.at[r - 1, i]))

                seen = seen + mine.astype(jnp.int32)

    each(lambda c: c.start())
    each(lambda c: c.wait())


def route(me, pool, tables, factor):
    per_owner, rank, width = factor.shape
    groups = len(tables) + 1
    return pl.pallas_call(
        functools.partial(route_kernel, per_owner),
        out_shape=jax.ShapeDtypeStruct((groups, OWNER_CAP, rank, width), factor.dtype),
        in_specs=[pl.BlockSpec(memory_space=pltpu.SMEM)] * (groups + 1) + [pl.BlockSpec(memory_space=pltpu.VMEM)],
        out_specs=pl.BlockSpec(memory_space=pl.ANY),
        scratch_shapes=[pltpu.SemaphoreType.DMA((groups - 1, tables[0].shape[1]))],
        compiler_params=params(62),
        cost_estimate=cost(0, 2 * (per_owner + groups * OWNER_CAP) * rank * width),
        name="adapters_to_send",
    )(me, pool, *tables, factor)


def fetch(me_ref, pool_ref, own_table, own_ref, got_ref, held, sems):
    per_owner, tiles = own_ref.shape[0], own_table.shape[1]
    slots = [pool_ref[own_table[0, i]] for i in range(tiles)]
    me = me_ref[0]
    for i in range(tiles):
        owner = slots[i] // per_owner
        place = jnp.int32(0)
        for k in range(i):
            place = place + (slots[k] // per_owner == owner).astype(jnp.int32)

        @pl.when(owner == me)
        def _(i=i):
            pltpu.make_async_copy(own_ref.at[slots[i] % per_owner], held.at[i], sems.at[i]).start()

        @pl.when(owner != me)
        def _(i=i, owner=owner, place=place):
            pltpu.make_async_copy(got_ref.at[owner, place], held.at[i], sems.at[i]).start()


def rank_kernel(me_ref, pool_ref, own_table, hidden_ref, own_ref, got_ref, out_ref, rows_ref, held, row_sems, sems):
    tiles = own_table.shape[1]
    rows = rows_ref.shape[1]

    def tile_copy(i):
        return pltpu.make_async_copy(hidden_ref.at[pl.ds(i * rows, rows)], rows_ref.at[i], row_sems.at[i])

    for i in range(tiles):
        tile_copy(i).start()
    fetch(me_ref, pool_ref, own_table, own_ref, got_ref, held, sems)
    for i in range(tiles):
        tile_copy(i).wait()
        pltpu.make_async_copy(own_ref.at[0], held.at[i], sems.at[i]).wait()
        out_ref[i] = lax.dot_general(
            held[i], rows_ref[i], (((1,), (1,)), ((), ())), preferred_element_type=jnp.float32
        ).astype(jnp.bfloat16)


def rank_values(me, pool, table, hidden, own, got):
    _, rank, width = own.shape
    tiles = table.shape[1]
    rows = hidden.shape[0] // tiles
    return pl.pallas_call(
        rank_kernel,
        out_shape=jax.ShapeDtypeStruct((tiles, rank, rows), jnp.bfloat16),
        in_specs=[pl.BlockSpec(memory_space=pltpu.SMEM)] * 3 + [pl.BlockSpec(memory_space=pl.ANY)] * 3,
        out_specs=pl.BlockSpec(memory_space=pltpu.VMEM),
        scratch_shapes=[
            pltpu.VMEM((tiles, rows, width), jnp.bfloat16),
            pltpu.VMEM((tiles, rank, width), jnp.bfloat16),
            pltpu.SemaphoreType.DMA((tiles,)),
            pltpu.SemaphoreType.DMA((tiles,)),
        ],
        compiler_params=params(62),
        cost_estimate=cost(2 * hidden.size * rank, 2 * (hidden.size + tiles * rank * width)),
        name="rank_values",
    )(me, pool, table, hidden, own, got)


def sum_kernel(n_add, chunks, *refs):
    adds, out_ref = refs[: n_add * chunks], refs[-1] if len(refs) == n_add * chunks + 1 else refs[-2]
    width = adds[0].shape[2]
    for c in range(chunks):
        value = adds[c * n_add][0].astype(jnp.float32)
        for add in adds[c * n_add + 1 : (c + 1) * n_add]:
            value = value + add[0].astype(jnp.float32)
        out_ref[:, pl.ds(c * width, width)] = value.astype(out_ref.dtype)
    if len(refs) > n_add * chunks + 1:
        ranks, rank_ref = refs[n_add * chunks : -2], refs[-1]
        for t in range(rank_ref.shape[0]):
            rank = ranks[0][t].astype(jnp.float32)
            for other in ranks[1:]:
                rank = rank + other[t].astype(jnp.float32)
            rank_ref[t] = rank.astype(jnp.bfloat16).T


def sum_base(adds, tiles, per_step, ranks=()):
    flat = [a for chunk in adds for a in chunk]
    _, tokens, n_cols = flat[0].shape
    steps = tiles // per_step
    rows = tokens // steps
    width = n_cols * len(adds)
    out_shape = [jax.ShapeDtypeStruct((tokens, width), jnp.bfloat16)]
    out_specs = [pl.BlockSpec((rows, width), lambda i: (i, 0))]
    rank_specs = []
    for part in ranks:
        rank_specs.append(pl.BlockSpec((per_step, *part.shape[1:]), lambda i: (i, 0, 0)))
    if ranks:
        _, rank, tile = ranks[0].shape
        out_shape.append(jax.ShapeDtypeStruct((tiles, tile, rank), jnp.bfloat16))
        out_specs.append(pl.BlockSpec((per_step, tile, rank), lambda i: (i, 0, 0)))
    return pl.pallas_call(
        functools.partial(sum_kernel, len(adds[0]), len(adds)),
        out_shape=out_shape,
        grid=(steps,),
        in_specs=[pl.BlockSpec((1, rows, n_cols), lambda i: (0, i, 0))] * len(flat) + rank_specs,
        out_specs=out_specs,
        compiler_params=params(62),
        cost_estimate=cost(tokens * n_cols * len(flat), tokens * (2 * n_cols * len(flat) + 2 * width)),
        name="base_sum",
    )(*flat, *ranks)


def final_kernel(per_step, me_ref, pool_ref, own_table, base_ref, last_ref, rank_ref, own_ref, got_ref, out_ref, held, sems):
    step = pl.program_id(0)
    rows = rank_ref.shape[1]
    summed = base_ref.shape[1]

    @pl.when(step == 0)
    def _():
        fetch(me_ref, pool_ref, own_table, own_ref, got_ref, held, sems)

    for t in range(per_step):
        tile = step * per_step + t
        span = pl.ds(t * rows, rows)
        pltpu.make_async_copy(own_ref.at[0], held.at[tile], sems.at[tile]).wait()
        adapted = jnp.dot(rank_ref[t], held[tile], preferred_element_type=jnp.float32)
        adapted = (adapter_scale * adapted).astype(jnp.bfloat16).astype(jnp.float32)
        out_ref[span, pl.ds(0, summed)] = (base_ref[span, :].astype(jnp.float32) + adapted[:, :summed]).astype(jnp.bfloat16)
        rest = last_ref[span, :].astype(jnp.float32) + adapted[:, summed:]
        out_ref[span, pl.ds(summed, rest.shape[1])] = rest.astype(jnp.bfloat16)


def final(me, pool, table, ranks, base, last, own, got):
    _, rank, width = own.shape
    tiles, rows, _ = ranks.shape
    per_step = 4
    step_rows = per_step * rows
    return pl.pallas_call(
        functools.partial(final_kernel, per_step),
        out_shape=jax.ShapeDtypeStruct((tiles * rows, width), jnp.bfloat16),
        grid=(tiles // per_step,),
        in_specs=[pl.BlockSpec(memory_space=pltpu.SMEM)] * 3
        + [pl.BlockSpec((step_rows, a.shape[1]), lambda i: (i, 0)) for a in (base, last)]
        + [pl.BlockSpec((per_step, rows, rank), lambda i: (i, 0, 0))]
        + [pl.BlockSpec(memory_space=pl.ANY)] * 2,
        out_specs=pl.BlockSpec((step_rows, width), lambda i: (i, 0)),
        scratch_shapes=[
            pltpu.VMEM((tiles, rank, width), jnp.bfloat16),
            pltpu.SemaphoreType.DMA((tiles,)),
        ],
        compiler_params=params(62),
        cost_estimate=cost(2 * tiles * rows * rank * width, 4 * tiles * rows * width),
        name="adapted_and_sum",
    )(me, pool, table, base, last, ranks, own, got)


def local(
    groups,
    n_tp,
    hidden,
    down_weight,
    adapter_down_factor,
    adapter_up_factor,
    row_tile_adapter,
    adapter_pool_slot,
):
    chips = n_tp // 2
    width = down_weight.shape[1] // n_tp
    chunks = max(1, min(CHUNKS, width // 128))
    n_cols = width // chunks
    tile = min(512, n_cols)
    grp, tp = lax.axis_index("grp"), lax.axis_index("tp")
    chip, core = tp // 2, tp % 2
    me = grp.reshape(1).astype(jnp.int32)

    pool = adapter_pool_slot.astype(jnp.int32)
    own_table = row_tile_adapter.reshape(1, -1).astype(jnp.int32)
    tables = [lax.ppermute(own_table, "grp", [(g, g ^ r) for g in range(groups)]) for r in range(1, groups)]

    def send(v):
        return lax.all_to_all(v, "grp", 0, 0, tiled=True)

    down_out = route(me, pool, tables, adapter_down_factor)
    down_in = send(down_out)

    relative = jnp.array(list(range(1, chips)) + [0], jnp.int32)
    far_chips = (chip ^ relative).astype(jnp.int32)
    theirs, ours = far_chips * 2 + (1 - core), far_chips * 2 + core
    done = down_out
    others, adds = {}, []

    def first_core(c, *done):
        (first,) = gemm(hidden, down_weight, after(theirs, *done), width, n_cols, c * n_cols, tile, chips)
        others[c] = lax.ppermute(first, "tp", [(i, i ^ 1) for i in range(n_tp)])
        return first

    done = first_core(0, down_out)
    for c in range(chunks):
        earlier = adds[c - 2] if c >= 2 else []
        if c + 1 < chunks:
            done = first_core(c + 1, done, *earlier)
        if c == chunks - 1:
            up_out = route(after(me, done), pool, tables, adapter_up_factor)
            done = up_out
        sums = gemm(hidden, down_weight, after(ours, done, *earlier), width, n_cols, c * n_cols, tile, 1, (others[c],))
        done = sums[chips - 1]
        got = [
            lax.ppermute(sums[r - 1], "tp", [(i, i ^ (2 * r)) for i in range(n_tp)])
            for r in range(1, chips)
        ]
        adds.append([done] + got)
    up_in = send(after(up_out, done, *sum(adds[:-2], []), *adds[-2][:UP_GATE]))

    ranks = rank_values(after(me, done), pool, own_table, hidden, adapter_down_factor, down_in)
    ranks = ranks + lax.ppermute(ranks, "tp", [(i, i ^ 1) for i in range(n_tp)])
    ranks = [ranks] + [lax.ppermute(ranks, "tp", [(i, i ^ (2 * r)) for i in range(n_tp)]) for r in range(1, chips)]

    tiles = own_table.shape[1]
    (base,) = sum_base(adds[:-1], tiles, 2)
    last, ranks = sum_base(adds[-1:], tiles, 4, ranks)
    return final(me, pool, own_table, ranks, base, last, adapter_up_factor, up_in)


def solution(mesh):
    placed = (
        P("grp", "tp"),
        P("tp", None),
        P("grp", None, "tp"),
        P("grp", None, "tp"),
        P("grp"),
        P(),
    )
    return jax.shard_map(
        functools.partial(local, mesh.shape["grp"], mesh.shape["tp"]),
        mesh=mesh,
        in_specs=placed,
        out_specs=P("grp", "tp"),
        check_vma=False,
    )
```
